32 devices in a mesh: epoch: 32 (over z, y, x, core), param: 1.
Axes of the slice: x: 2, y: 2, z: 4, core: 2. Of those that a mesh axis runs over, the one named last changes fastest.
Arguments:
- initial_carry: float32 [48, 8192], P(None, 'param'), may hold values from -6 to 6
- forcing: bfloat16 [128, 48, 8192], P('epoch', None, 'param'), may hold values from -2.390625 to 2.390625
- transition: float32 [128, 6, 6, 8], P('epoch'), may hold values from -0.2 to 1.2
- partials: float32 [6, 4096], P(None, 'epoch'), may hold values from -40 to 40
- arc_of_row: int32 [4096], P('epoch'), may hold values from 0 to 7
- counts: int32 [128], P('epoch'), may hold values from 8 to 32
Outputs:
- packed: float32 [4096, 8192], P('epoch', 'param')
- r_rows: float32 [512, 8192], P(None, 'param')
The draws below stay inside these ranges and needn't reach their ends.
Inputs may be any that keep to these rules, and one draw needn't show every extreme that they name: Rows of block j at positions counts[j] and beyond carry no observation.
All inputs are finite; a program needn't handle non-finite values.
Results may differ from the reference program's by a relative error of at most 0.0003.
Values sent between devices are 32-bit elements; how exact they have to be, the bound alone decides.
A program may use at most 128 MiB of HBM per device.

```python
import math
import jax
import jax.numpy as jnp
from jax import lax

PARAMS = 8192
PANEL = 256
STATE = 6
ARCS = 8
BLOCK_ROWS = 32
TIME_SPAN_COUNT = 128
ROWS = 4096
ARC_ROWS = 48


def draw_transition(key, part):
    partial_derivative_transfers = jax.random.split(key, 6)
    slow_share = 0.5
    slow_arcs = jax.random.uniform(partial_derivative_transfers[0], (ARCS,)) < slow_share
    strength = jax.random.uniform(partial_derivative_transfers[1], (ARCS,), minval=0.1, maxval=0.4)
    jitter = jax.random.uniform(partial_derivative_transfers[2], (TIME_SPAN_COUNT, ARCS), minval=0.5, maxval=1.5)
    slow_decay = jnp.exp(jnp.log(0.1) * strength[None, :] * jitter / TIME_SPAN_COUNT)
    fast_decay = jax.random.uniform(partial_derivative_transfers[3], (TIME_SPAN_COUNT, ARCS), minval=0.3, maxval=0.6)
    damping_multipliers = jnp.where(slow_arcs[None, :], slow_decay, fast_decay)
    pulse_first_offset = jax.random.randint(partial_derivative_transfers[4], (3,), 0, TIME_SPAN_COUNT)
    pulse_line_cluster = jnp.any(jnp.arange(TIME_SPAN_COUNT)[:, None] == pulse_first_offset[None, :], axis=1)
    damping_multipliers = damping_multipliers * jnp.where(pulse_line_cluster, 0.7, 1.0)[:, None]
    perturb = jnp.clip(jax.random.normal(partial_derivative_transfers[5], (TIME_SPAN_COUNT, STATE, STATE, ARCS)), -4.0, 4.0)
    identity_block = jnp.eye(STATE, dtype=jnp.float32)[None, :, :, None]
    return damping_multipliers[:, None, None, :] * (identity_block + 0.1 / jnp.sqrt(6.0) * perturb)


def draw_partials(key, part):
    partial_derivative_transfers = jax.random.split(key, 2)
    row_scale = jnp.exp(jax.random.uniform(partial_derivative_transfers[0], (1, ROWS), minval=0.0, maxval=jnp.log(10.0)))
    values = jnp.clip(jax.random.normal(partial_derivative_transfers[1], (STATE, ROWS)), -4.0, 4.0)
    return values * row_scale


def plant(drawn, stream_key, smallest, top_value):
    spot = [jax.random.randint(jax.random.fold_in(stream_key, axis), (), 0, length) for axis, length in enumerate(drawn.shape)]
    main_axis = drawn.shape.index(max(drawn.shape))
    neighbour = spot[:main_axis] + [(spot[main_axis] + 1) % drawn.shape[main_axis]] + spot[main_axis + 1:]
    return drawn.at[tuple(spot)].set(smallest).at[tuple(neighbour)].set(top_value)


def levels(key, dims, cuts, least, high):
    gain = 1.0
    for dim, shards_of in cuts:
        steps = jax.random.uniform(jax.random.fold_in(jax.random.fold_in(key, 6), dim), (shards_of,), jnp.float32, least / len(cuts), high / len(cuts))
        gain = gain * jnp.repeat(jnp.exp(steps), dims[dim] // shards_of).reshape((-1,) + (1,) * (len(dims) - 1 - dim))
    return gain


def centred(own_key, shape, width, reach, cuts=(), kind=jnp.bfloat16):
    drawn = jax.random.normal(own_key, shape, jnp.float32) * width
    if len(cuts) > 0:
        drawn = levels(own_key, shape, cuts, -0.22, 0.18) * drawn
    return jnp.clip(drawn, min=-reach, max=reach).astype(kind)


def setup_inputs(seed: int = 0) -> dict:
    key_list = jax.random.split(jax.random.key(seed), 7)
    initial_carry = centred(key_list[0], (ARC_ROWS, PARAMS), 1.0, 6.0, (), jnp.float32)
    forcing = centred(key_list[1], (TIME_SPAN_COUNT, ARC_ROWS, PARAMS), 0.3, 2.390625, ((0, 32),))
    transition = draw_transition(jax.random.fold_in(key_list[6], 71), 0)
    partials = draw_partials(jax.random.fold_in(key_list[6], 71), 0)
    arc_of_row = plant(jax.random.randint(key_list[4], (ROWS,), 0, ARCS), jax.random.fold_in(key_list[4], 1), 0, ARCS - 1).astype(jnp.int32)
    counts = plant(jax.random.randint(key_list[5], (TIME_SPAN_COUNT,), BLOCK_ROWS // 4, BLOCK_ROWS + 1), jax.random.fold_in(key_list[5], 1), BLOCK_ROWS // 4, BLOCK_ROWS).astype(jnp.int32)
    return {"initial_carry": initial_carry, "forcing": forcing, "transition": transition, "partials": partials, "arc_of_row": arc_of_row, "counts": counts}


def propagate(carry, transition_step, driving_increment):
    states = transition_step.shape[0]
    view = carry.reshape(states, transition_step.shape[2], carry.shape[1])
    moved = jnp.einsum('cda,dap->cap', transition_step, view, precision=lax.Precision.HIGHEST)
    return moved.reshape(carry.shape) + driving_increment.astype(jnp.float32)

def observe(carry, partial_rows, orbit_track_lines, observed):
    arc_total = carry.shape[0] // partial_rows.shape[0]
    length = partial_rows.shape[1]
    live_rows = (jnp.arange(length) < observed).astype(jnp.float32)
    chosen = (orbit_track_lines[:, None] == jnp.arange(arc_total)[None, :]).astype(jnp.float32)
    weights = partial_rows.T[:, :, None] * chosen[:, None, :] * live_rows[:, None, None]
    return jnp.dot(weights.reshape(length, carry.shape[0]), carry, precision=lax.Precision.HIGHEST)

def reduce_panel(matrix, panel_cols):
    products = jnp.dot(panel_cols.T, matrix, precision=lax.Precision.HIGHEST)
    gram_block = jnp.dot(panel_cols.T, panel_cols, precision=lax.Precision.HIGHEST)
    factor = jnp.linalg.cholesky(gram_block)
    row_block = jax.scipy.linalg.solve_triangular(factor, products, lower=True)
    orthonormal = jax.scipy.linalg.solve_triangular(factor, panel_cols.T, lower=True).T
    updated = matrix - jnp.dot(orthonormal, row_block, precision=lax.Precision.HIGHEST)
    return (updated, row_block, orthonormal)

def reference(initial_carry, forcing, transition, partials, arc_of_row, counts):
    block_partials = partials.reshape(STATE, TIME_SPAN_COUNT, BLOCK_ROWS).transpose(1, 0, 2)
    block_arcs = arc_of_row.reshape(TIME_SPAN_COUNT, BLOCK_ROWS)

    def advance(carry, inputs):
        driving_increment, transition_step, partial_rows, orbit_track_lines, observed = inputs
        carry = propagate(carry, transition_step, driving_increment)
        return (carry, observe(carry, partial_rows, orbit_track_lines, observed))
    closing_carry_state, stacked = lax.scan(advance, initial_carry, (forcing, transition, block_partials, block_arcs, counts))
    matrix = stacked.reshape(ROWS, PARAMS)
    row_parts = []
    basis_parts = []
    for number in range(2):
        panel_cols = matrix[:, number * PANEL:(number + 1) * PANEL]
        matrix, row_block, orthonormal = reduce_panel(matrix, panel_cols)
        row_parts.append(row_block)
        basis_parts.append(orthonormal)
    root_rows = math.sqrt(ROWS)
    head_cols = jnp.concatenate(basis_parts, 1) * root_rows
    packed = jnp.concatenate([head_cols, matrix[:, 2 * PANEL:]], 1)
    r_rows = jnp.concatenate(row_parts, 0) / root_rows
    return (packed, r_rows)
```

```python
import functools
import math

import jax
import jax.numpy as jnp
from jax import lax
from jax.experimental import pallas as pl
from jax.experimental.pallas import tpu as pltpu
from jax.sharding import PartitionSpec as P

PANEL = 256
HIGH = lax.Precision.HIGHEST


def dot(a, b):
    return jnp.dot(a, b, precision=HIGH, preferred_element_type=jnp.float32)


def dot_t(a, b):
    return lax.dot_general(
        a, b, (((0,), (0,)), ((), ())), precision=HIGH, preferred_element_type=jnp.float32
    )


def scan_kernel(states, arcs, start_ref, map_ref, shift_ref, out_ref):
    count, _, width = shift_ref.shape
    lanes = map_ref.shape[-1]
    for left in range(0, width, lanes):
        cols = slice(left, left + lanes)
        first = tuple(start_ref[d * arcs : (d + 1) * arcs, cols] for d in range(states))

        def step(p, carry):
            after = []
            for c in range(states):
                rows = pl.ds(c * arcs, arcs)
                out_ref[p, rows, cols] = carry[c]
                total = shift_ref[p, rows, cols]
                for d in range(states):
                    total = total + map_ref[p, c * states + d] * carry[d]
                after.append(total)
            return tuple(after)

        lax.fori_loop(0, count, step, first)


def entering(start, maps, shifts, states, arcs):
    count, rows, width = shifts.shape
    lanes = min(width, 128)
    spread_maps = jnp.broadcast_to(
        maps.reshape(count, states * states, arcs, 1), (count, states * states, arcs, lanes)
    )
    return pl.pallas_call(
        functools.partial(scan_kernel, states, arcs),
        out_shape=jax.ShapeDtypeStruct(shifts.shape, jnp.float32),
        in_specs=[pl.BlockSpec(memory_space=pltpu.VMEM)] * 3,
        out_specs=pl.BlockSpec(memory_space=pltpu.VMEM),
        compiler_params=pltpu.CompilerParams(vmem_limit_bytes=40 << 20),
        cost_estimate=pl.CostEstimate(
            flops=2 * states * count * rows * width,
            bytes_accessed=8 * count * rows * width,
            transcendentals=0,
        ),
    )(start, spread_maps, shifts)


def from_first_shard(block):
    if lax.axis_size("param") == 1:
        return block
    block = jnp.where(lax.axis_index("param") == 0, block, jnp.zeros_like(block))
    return lax.psum(block, "param")


def lower_inverse(factor):
    unit = jnp.eye(factor.shape[0], dtype=jnp.float32)
    return jax.scipy.linalg.solve_triangular(factor, unit, lower=True)


def local(initial_carry, forcing, transition, partials, arc_of_row, counts):
    blocks, states, _, arcs = transition.shape
    carried, width = initial_carry.shape
    rows = partials.shape[1]
    length = rows // blocks
    epochs = lax.axis_size("epoch")
    share = width // epochs
    place = lax.axis_index("epoch")

    same = jnp.eye(arcs, dtype=jnp.float32)
    dense = (
        transition.transpose(0, 1, 3, 2)[..., None] * same[None, None, :, None, :]
    ).reshape(blocks, carried, carried)
    live = jnp.arange(length)[None, :] < counts[:, None]
    chosen = (arc_of_row[:, None] == jnp.arange(arcs)[None, :]).astype(jnp.float32)
    weights = (
        partials.T[:, :, None] * chosen[:, None, :] * live.reshape(rows, 1, 1).astype(jnp.float32)
    ).reshape(rows, carried)
    reach = jnp.eye(carried, dtype=jnp.float32)
    columns = []
    for k in range(blocks - 1, -1, -1):
        reach = jnp.concatenate([weights[k * length : (k + 1) * length], reach], 0)
        columns.insert(
            0, jnp.concatenate([jnp.zeros((k * length, carried), jnp.float32), reach], 0)
        )
        reach = dot(reach, dense[k])
    sources = jnp.concatenate(columns, 1)
    view, summary = reach[:rows], reach[rows:]
    summary = jnp.sum(
        summary.reshape(states, arcs, states, arcs) * same[None, :, None, :], 3
    ).transpose(0, 2, 1)

    own = dot(sources, forcing.reshape(blocks * carried, width).astype(jnp.float32))
    own_design, own_shift = own[:rows], own[rows:]

    head = 2 * PANEL
    first = from_first_shard(own[:, :head])
    first_start = from_first_shard(initial_carry[:, :head])
    flat = jnp.concatenate([view.reshape(-1), summary.reshape(-1)])
    extra = -(-flat.size // (8 * head)) * 8
    flat = jnp.pad(flat, (0, extra * head - flat.size)).reshape(extra, head)
    every = lax.all_gather(jnp.concatenate([first, flat], 0), "epoch")

    tail = -(-summary.size // (8 * share)) * 8
    packed_map = jnp.pad(summary.reshape(-1), (0, tail * share - summary.size))
    outgoing = jnp.concatenate(
        [
            own_shift.reshape(carried, epochs, share).transpose(1, 0, 2),
            jnp.broadcast_to(packed_map.reshape(1, tail, share), (epochs, tail, share)),
        ],
        1,
    )
    arrived = lax.all_to_all(outgoing, "epoch", 0, 0)
    maps = arrived[:, carried:].reshape(epochs, -1)[:, : summary.size]
    maps = maps.reshape(epochs, states, states, arcs)
    start = lax.dynamic_slice_in_dim(initial_carry, place * share, share, 1)
    before = entering(start, maps, arrived[:, :carried], states, arcs)
    incoming = lax.all_to_all(before, "epoch", 0, 0)
    incoming = incoming.transpose(1, 0, 2).reshape(carried, width)
    design = own_design + dot(view, incoming)

    shares = lax.all_to_all(
        design.reshape(rows, epochs, share).transpose(1, 0, 2), "epoch", 0, 0
    ).reshape(epochs * rows, share)

    tails = every[:, rows + carried :].reshape(epochs, -1)
    views = tails[:, : view.size].reshape(epochs, rows, carried)
    all_maps = tails[:, view.size : view.size + summary.size]
    all_maps = all_maps.reshape(epochs, states, states, arcs)
    first_in = entering(first_start, all_maps, every[:, rows : rows + carried], states, arcs)
    panels = every[:, :rows] + jnp.einsum(
        "prk,pkc->prc", views, first_in, precision=HIGH, preferred_element_type=jnp.float32
    )
    panels = panels.reshape(epochs * rows, head)
    gram = dot_t(panels, panels)
    inverse0 = lower_inverse(jnp.linalg.cholesky(gram[:PANEL, :PANEL]))
    cross = dot(inverse0, gram[:PANEL, PANEL:])
    inverse1 = lower_inverse(jnp.linalg.cholesky(gram[PANEL:, PANEL:] - dot_t(cross, cross)))

    products = dot_t(panels, shares)
    upper = dot(inverse0, products[:PANEL])
    lower = dot(inverse1, products[PANEL:] - dot_t(cross, upper))
    r_rows = lax.all_gather(jnp.concatenate([upper, lower], 0), "epoch", axis=1, tiled=True)

    mine = from_first_shard(design[:, :head])
    basis0 = dot(mine[:, :PANEL], inverse0.T)
    basis1 = dot(mine[:, PANEL:] - dot(basis0, cross), inverse1.T)
    basis = jnp.concatenate([basis0, basis1], 1)

    root_rows = math.sqrt(epochs * rows)
    if lax.axis_size("param") == 1:
        rest = design[:, head:] - dot(basis, r_rows[:, head:])
        front = basis * root_rows
    else:
        matrix = design - dot(basis, r_rows)
        rest = matrix[:, head:]
        front = jnp.where(lax.axis_index("param") == 0, basis * root_rows, matrix[:, :head])
    return jnp.concatenate([front, rest], 1), r_rows / root_rows


def solution(mesh):
    placed = (
        P(None, "param"),
        P("epoch", None, "param"),
        P("epoch", None, None, None),
        P(None, "epoch"),
        P("epoch"),
        P("epoch"),
    )
    return jax.shard_map(
        local,
        mesh=mesh,
        in_specs=placed,
        out_specs=(P("epoch", "param"), P(None, "param")),
        check_vma=False,
    )
```

```python
import functools
import math

import jax
import jax.numpy as jnp
from jax import lax
from jax.experimental import pallas as pl
from jax.experimental.pallas import tpu as pltpu
from jax.sharding import PartitionSpec as P

PANEL = 256
HIGH = lax.Precision.HIGHEST


def dot(a, b):
    return jnp.dot(a, b, precision=HIGH, preferred_element_type=jnp.float32)


def dot_t(a, b):
    return lax.dot_general(
        a, b, (((0,), (0,)), ((), ())), precision=HIGH, preferred_element_type=jnp.float32
    )


def scan_kernel(states, arcs, start_ref, map_ref, shift_ref, out_ref):
    count, _, width = shift_ref.shape
    lanes = map_ref.shape[-1]
    for left in range(0, width, lanes):
        cols = slice(left, left + lanes)
        first = tuple(start_ref[d * arcs : (d + 1) * arcs, cols] for d in range(states))

        def step(p, carry):
            after = []
            for c in range(states):
                rows = pl.ds(c * arcs, arcs)
                out_ref[p, rows, cols] = carry[c]
                total = shift_ref[p, rows, cols]
                for d in range(states):
                    total = total + map_ref[p, c * states + d] * carry[d]
                after.append(total)
            return tuple(after)

        lax.fori_loop(0, count, step, first)


def entering(start, maps, shifts, states, arcs):
    count, rows, width = shifts.shape
    lanes = min(width, 128)
    spread_maps = jnp.broadcast_to(
        maps.reshape(count, states * states, arcs, 1), (count, states * states, arcs, lanes)
    )
    return pl.pallas_call(
        functools.partial(scan_kernel, states, arcs),
        out_shape=jax.ShapeDtypeStruct(shifts.shape, jnp.float32),
        in_specs=[pl.BlockSpec(memory_space=pltpu.VMEM)] * 3,
        out_specs=pl.BlockSpec(memory_space=pltpu.VMEM),
        compiler_params=pltpu.CompilerParams(vmem_limit_bytes=40 << 20),
        cost_estimate=pl.CostEstimate(
            flops=2 * states * count * rows * width,
            bytes_accessed=8 * count * rows * width,
            transcendentals=0,
        ),
    )(start, spread_maps, shifts)


def from_first_shard(block):
    if lax.axis_size("param") == 1:
        return block
    block = jnp.where(lax.axis_index("param") == 0, block, jnp.zeros_like(block))
    return lax.psum(block, "param")


def lower_inverse(factor):
    unit = jnp.eye(factor.shape[0], dtype=jnp.float32)
    return jax.scipy.linalg.solve_triangular(factor, unit, lower=True)


def factored(gram):
    size = gram.shape[0]
    half = size // 2
    inverse_a = lower_inverse(jnp.linalg.cholesky(gram[:half, :half]))
    upper_a = dot(inverse_a, gram[:half])
    side = upper_a[:, half:size]
    left = gram[half:] - dot_t(side, upper_a)
    inverse_b = lower_inverse(jnp.linalg.cholesky(left[:, half:size]))
    upper_b = dot(inverse_b, left)
    corner = -dot(inverse_b, dot_t(side, inverse_a))
    inverse = jnp.concatenate(
        [
            jnp.concatenate([inverse_a, jnp.zeros((half, size - half), jnp.float32)], 1),
            jnp.concatenate([corner, inverse_b], 1),
        ],
        0,
    )
    return inverse, jnp.concatenate([upper_a, upper_b], 0)


def local(initial_carry, forcing, transition, partials, arc_of_row, counts):
    blocks, states, _, arcs = transition.shape
    carried, width = initial_carry.shape
    rows = partials.shape[1]
    length = rows // blocks
    epochs = lax.axis_size("epoch")
    share = width // epochs
    place = lax.axis_index("epoch")

    same = jnp.eye(arcs, dtype=jnp.float32)
    dense = (
        transition.transpose(0, 1, 3, 2)[..., None] * same[None, None, :, None, :]
    ).reshape(blocks, carried, carried)
    live = jnp.arange(length)[None, :] < counts[:, None]
    chosen = (arc_of_row[:, None] == jnp.arange(arcs)[None, :]).astype(jnp.float32)
    weights = (
        partials.T[:, :, None] * chosen[:, None, :] * live.reshape(rows, 1, 1).astype(jnp.float32)
    ).reshape(rows, carried)
    reach = jnp.eye(carried, dtype=jnp.float32)
    columns = []
    for k in range(blocks - 1, -1, -1):
        reach = jnp.concatenate([weights[k * length : (k + 1) * length], reach], 0)
        columns.insert(
            0, jnp.concatenate([jnp.zeros((k * length, carried), jnp.float32), reach], 0)
        )
        reach = dot(reach, dense[k])
    sources = jnp.concatenate(columns, 1)
    view, summary = reach[:rows], reach[rows:]
    summary = jnp.sum(
        summary.reshape(states, arcs, states, arcs) * same[None, :, None, :], 3
    ).transpose(0, 2, 1)

    own = dot(sources, forcing.reshape(blocks * carried, width).astype(jnp.float32))
    own_design, own_shift = own[:rows], own[rows:]

    head = 2 * PANEL
    first = from_first_shard(own[:, :head])
    first_start = from_first_shard(initial_carry[:, :head])
    flat = jnp.concatenate([view.reshape(-1), summary.reshape(-1)])
    extra = -(-flat.size // (8 * head)) * 8
    flat = jnp.pad(flat, (0, extra * head - flat.size)).reshape(extra, head)
    every = lax.all_gather(jnp.concatenate([first, flat], 0), "epoch")

    tail = -(-summary.size // (8 * share)) * 8
    packed_map = jnp.pad(summary.reshape(-1), (0, tail * share - summary.size))
    outgoing = jnp.concatenate(
        [
            own_shift.reshape(carried, epochs, share).transpose(1, 0, 2),
            jnp.broadcast_to(packed_map.reshape(1, tail, share), (epochs, tail, share)),
        ],
        1,
    )
    arrived = lax.all_to_all(outgoing, "epoch", 0, 0)
    maps = arrived[:, carried:].reshape(epochs, -1)[:, : summary.size]
    maps = maps.reshape(epochs, states, states, arcs)
    start = lax.dynamic_slice_in_dim(initial_carry, place * share, share, 1)
    before = entering(start, maps, arrived[:, :carried], states, arcs)
    incoming = lax.all_to_all(before, "epoch", 0, 0)
    incoming = incoming.transpose(1, 0, 2).reshape(carried, width)
    design = own_design + dot(view, incoming)

    shares = lax.all_to_all(
        design.reshape(rows, epochs, share).transpose(1, 0, 2), "epoch", 0, 0
    ).reshape(epochs * rows, share)

    tails = every[:, rows + carried :].reshape(epochs, -1)
    views = tails[:, : view.size].reshape(epochs, rows, carried)
    all_maps = tails[:, view.size : view.size + summary.size]
    all_maps = all_maps.reshape(epochs, states, states, arcs)
    first_in = entering(first_start, all_maps, every[:, rows : rows + carried], states, arcs)
    panels = every[:, :rows] + jnp.einsum(
        "prk,pkc->prc", views, first_in, precision=HIGH, preferred_element_type=jnp.float32
    )
    panels = panels.reshape(epochs * rows, head)
    gram = dot_t(panels, panels)
    inverse0, upper0 = factored(gram[:PANEL])
    cross = upper0[:, PANEL:]
    inverse1, _ = factored(gram[PANEL:, PANEL:] - dot_t(cross, cross))

    products = dot_t(panels, shares)
    upper = dot(inverse0, products[:PANEL])
    lower = dot(inverse1, products[PANEL:] - dot_t(cross, upper))
    r_rows = lax.all_gather(jnp.concatenate([upper, lower], 0), "epoch", axis=1, tiled=True)

    mine = from_first_shard(design[:, :head])
    basis0 = dot(mine[:, :PANEL], inverse0.T)
    basis1 = dot(mine[:, PANEL:] - dot(basis0, cross), inverse1.T)
    basis = jnp.concatenate([basis0, basis1], 1)

    root_rows = math.sqrt(epochs * rows)
    if lax.axis_size("param") == 1:
        rest = design[:, head:] - dot(basis, r_rows[:, head:])
        front = basis * root_rows
    else:
        matrix = design - dot(basis, r_rows)
        rest = matrix[:, head:]
        front = jnp.where(lax.axis_index("param") == 0, basis * root_rows, matrix[:, :head])
    return jnp.concatenate([front, rest], 1), r_rows / root_rows


def solution(mesh):
    placed = (
        P(None, "param"),
        P("epoch", None, "param"),
        P("epoch", None, None, None),
        P(None, "epoch"),
        P("epoch"),
        P("epoch"),
    )
    return jax.shard_map(
        local,
        mesh=mesh,
        in_specs=placed,
        out_specs=(P("epoch", "param"), P(None, "param")),
        check_vma=False,
    )
```
